32 devices in a mesh: group: 2 (over y), seq: 8 (over z, x), mp: 2 (over core).
Axes of the slice: x: 2, y: 2, z: 4, core: 2. Of those that a mesh axis runs over, the one named last changes fastest.
Arguments:
- student_hidden: bfloat16 [2, 1024, 3072], P('group', 'seq', 'mp'), may hold values from -6 to 6
- student_cond: float32 [2, 3072], P(None, 'seq'), may hold values from -6 to 6
- student_mod: bfloat16 [3072, 2, 3072], P('seq', 'group', 'mp'), may hold values from -0.109375 to 0.109375
- student_out: bfloat16 [3072, 64], P('mp'), may hold values from -0.109375 to 0.109375
- timestep: int32 [2], P('group'), may hold values from 0 to 999
- noise: bfloat16 [2, 1024, 64], P('group', 'seq'), may hold values from -6 to 6
- teacher_embed: bfloat16 [64, 3072], P(None, 'mp'), may hold values from -0.75 to 0.75
- teacher_mod: bfloat16 [256, 2, 3072], P(None, None, 'mp'), may hold values from -0.375 to 0.375
- up_weight: bfloat16 [3072, 6144], P('seq', 'mp'), may hold values from -0.109375 to 0.109375
- down_weight: bfloat16 [6144, 3072], P('mp', 'seq'), may hold values from -0.078125 to 0.078125
- head_proj: bfloat16 [4, 3072, 128], P(None, 'mp'), may hold values from -0.109375 to 0.109375
- head_kernel: float32 [4, 3, 3, 128], replicated, may hold values from -3 to 3
- head_out: float32 [4, 128], replicated, may hold values from -2 to 2
- disc_layer: int32 [2, 4], P('group'), may hold values from 0 to 1, as said below
Outputs:
- latents: bfloat16 [2, 1024, 64], P('group', 'seq')
- logits: float32 [2, 4, 1024], P('group', None, 'seq')
- latent_grad: float32 [2, 1024, 64], P('group', 'seq')
The draws below stay inside these ranges and needn't reach their ends.
Inputs may be any that keep to these rules, and one draw needn't show every extreme that they name: `disc_layer`: for every sample, exactly half of the 4 heads read layer 0 and the other half layer 1, in an order drawn afresh.
All inputs are finite; a program needn't handle non-finite values.
Results may differ from the reference program's by a relative error of at most 0.029.
Values may be sent and summed in bfloat16 or wider, within the bound.
A program may use at most 128 MiB of HBM per device.

```python
import math
import jax
import jax.numpy as jnp
from jax import lax

D = 3072
FFW = 6144
C = 64
FREQ = 256
HC = 128
HEADS = 4
GRID_W = 64
TOKENS = 1024
SAMPLES = 2


def draw_disc_layer(key, part):
    keys = jax.random.split(jax.random.fold_in(key, 17), SAMPLES)
    base_row = jnp.arange(HEADS, dtype=jnp.int32) % 2
    return jax.vmap(lambda row_key: jax.random.permutation(row_key, base_row))(keys)


def block_levels(key, dims, shards, low, high):
    level = 1.0
    for dim, blocks in shards:
        steps = jax.random.uniform(jax.random.fold_in(jax.random.fold_in(key, 6), dim), (blocks,), jnp.float32, low / len(shards), high / len(shards))
        level = level * jnp.repeat(jnp.exp(steps), dims[dim] // blocks).reshape((-1,) + (1,) * (len(dims) - 1 - dim))
    return level


def normal_values(key, extent, deviation, limit, cuts=(), held_as=jnp.bfloat16):
    result = deviation * jax.random.normal(key, extent, jnp.float32)
    if cuts:
        result = result * block_levels(key, extent, cuts, -0.22, 0.18)
    return jnp.clip(result, -limit, limit).astype(held_as)


def setup_inputs(seed: int = 0) -> dict:
    key_list = jax.random.split(jax.random.key(seed), 15)
    return {
        "student_hidden": normal_values(key_list[0], (SAMPLES, TOKENS, D), 1.0, 6.0, ((0, 2), (1, 8), (2, 2))),
        "student_cond": normal_values(key_list[1], (SAMPLES, D), 1.0, 6.0, ((1, 8),), jnp.float32),
        "student_mod": normal_values(key_list[2], (D, 2, D), D ** -0.5, 0.109375, ((0, 8), (1, 2), (2, 2))),
        "student_out": normal_values(key_list[3], (D, C), D ** -0.5, 0.109375, ((0, 2),)),
        "timestep": jax.random.randint(key_list[4], (SAMPLES,), 0, 1000).astype(jnp.int32),
        "noise": normal_values(key_list[5], (SAMPLES, TOKENS, C), 1.0, 6.0, ((0, 2), (1, 8))),
        "teacher_embed": normal_values(key_list[6], (C, D), C ** -0.5, 0.75, ((1, 2),)),
        "teacher_mod": normal_values(key_list[7], (FREQ, 2, D), FREQ ** -0.5, 0.375, ((2, 2),)),
        "up_weight": normal_values(key_list[8], (D, FFW), D ** -0.5, 0.109375, ((0, 8), (1, 2))),
        "down_weight": normal_values(key_list[9], (FFW, D), FFW ** -0.5, 0.078125, ((0, 2), (1, 8))),
        "head_proj": normal_values(key_list[10], (HEADS, D, HC), D ** -0.5, 0.109375, ((1, 2),)),
        "head_kernel": normal_values(key_list[11], (HEADS, 3, 3, HC), 0.5, 3.0, (), jnp.float32),
        "head_out": normal_values(key_list[12], (HEADS, HC), 0.3, 2.0, (), jnp.float32),
        "disc_layer": draw_disc_layer(jax.random.fold_in(key_list[14], 71), 0),
    }


EPSILON = 1e-06
GELU_COEF = 0.7978845608028654

def gelu_tanh(values):
    inner = GELU_COEF * (values + 0.044715 * values * values * values)
    return 0.5 * values * (1.0 + jnp.tanh(inner))

def gelu_slope(values):
    inner = GELU_COEF * (values + 0.044715 * values * values * values)
    tangent = jnp.tanh(inner)
    return 0.5 * (1.0 + tangent) + 0.5 * values * (1.0 - tangent * tangent) * GELU_COEF * (1.0 + 3.0 * 0.044715 * values * values)

def time_features(timestep, width):
    half_width = width // 2
    index = jnp.arange(half_width, dtype=jnp.float32)
    freqs = jnp.exp(-math.log(10000.0) * index / half_width)
    angles = timestep.astype(jnp.float32)[:, None] * freqs[None, :]
    return jnp.concatenate([jnp.cos(angles), jnp.sin(angles)], axis=-1)

def reference(student_hidden, student_cond, student_mod, student_out, timestep, noise, teacher_embed, teacher_mod, up_weight, down_weight, head_proj, head_kernel, head_out, disc_layer):
    highest = lax.Precision.HIGHEST
    hidden = student_hidden.astype(jnp.float32)
    tok_mean = lax.optimization_barrier(jnp.mean(hidden, -1, keepdims=True))
    tok_var = lax.optimization_barrier(jnp.mean((hidden - tok_mean) ** 2, -1, keepdims=True))
    smod = jnp.einsum('sk,kjd->sjd', student_cond, student_mod.astype(jnp.float32), precision=highest)
    normed = ((hidden - tok_mean) * lax.rsqrt(tok_var + EPSILON) * (1.0 + smod[:, 1:2]) + smod[:, 0:1]).astype(jnp.bfloat16)
    latents = jnp.einsum('std,dc->stc', normed.astype(jnp.float32), student_out.astype(jnp.float32), precision=highest).astype(jnp.bfloat16)
    level = timestep.astype(jnp.float32) / 1000.0
    retain = (1.0 - level)[:, None, None]
    noised = (retain * latents.astype(jnp.float32) + level[:, None, None] * noise.astype(jnp.float32)).astype(jnp.bfloat16)
    embedded = jnp.einsum('stc,cd->std', noised.astype(jnp.float32), teacher_embed.astype(jnp.float32), precision=highest).astype(jnp.bfloat16)
    tmod = jnp.einsum('sf,fjd->sjd', time_features(timestep, FREQ), teacher_mod.astype(jnp.float32), precision=highest)
    emb_f = embedded.astype(jnp.float32)
    mean_t = lax.optimization_barrier(jnp.mean(emb_f, -1, keepdims=True))
    var_t = lax.optimization_barrier(jnp.mean((emb_f - mean_t) ** 2, -1, keepdims=True))
    inv_std = lax.rsqrt(var_t + EPSILON)
    centered = (emb_f - mean_t) * inv_std
    mod_gain = 1.0 + tmod[:, 1:2]
    modulated = (centered * mod_gain + tmod[:, 0:1]).astype(jnp.bfloat16)
    preact = jnp.einsum('std,df->stf', modulated.astype(jnp.float32), up_weight.astype(jnp.float32), precision=highest)
    activated = gelu_tanh(preact).astype(jnp.bfloat16)
    block_out = (emb_f + jnp.einsum('stf,fd->std', activated.astype(jnp.float32), down_weight.astype(jnp.float32), precision=highest)).astype(jnp.bfloat16)
    layer_pick = disc_layer == 1
    head_w = head_proj.astype(jnp.float32)
    proj_embed = jnp.einsum('std,kdc->sktc', embedded.astype(jnp.float32), head_w, precision=highest)
    proj_block = jnp.einsum('std,kdc->sktc', block_out.astype(jnp.float32), head_w, precision=highest)
    projected = jnp.where(layer_pick[:, :, None, None], proj_block, proj_embed)
    grid_rows = TOKENS // GRID_W
    samples = projected.shape[0]
    grid = projected.reshape(samples, HEADS, grid_rows, GRID_W, HC)
    padded = jnp.pad(grid, ((0, 0), (0, 0), (1, 1), (1, 1), (0, 0)))
    conv_field = jnp.zeros(grid.shape, jnp.float32)
    for row_off in range(3):
        for col_off in range(3):
            conv_field = conv_field + head_kernel[:, row_off, col_off][None, :, None, None, :] * padded[:, :, row_off:row_off + grid_rows, col_off:col_off + GRID_W, :]
    gating = jax.nn.sigmoid(conv_field)
    weights_out = head_out[None, :, None, None, :]
    logits = lax.optimization_barrier(jnp.sum(conv_field * gating * weights_out, -1)).reshape(samples, HEADS, TOKENS)
    slope_grad = -weights_out * gating * (1.0 + conv_field * (1.0 - gating))
    padded_grad = jnp.pad(slope_grad, ((0, 0), (0, 0), (1, 1), (1, 1), (0, 0)))
    field_grad = jnp.zeros(grid.shape, jnp.float32)
    for row_off in range(3):
        for col_off in range(3):
            field_grad = field_grad + head_kernel[:, row_off, col_off][None, :, None, None, :] * padded_grad[:, :, 2 - row_off:2 - row_off + grid_rows, 2 - col_off:2 - col_off + GRID_W, :]
    field_grad = field_grad.reshape(samples, HEADS, TOKENS, HC).astype(jnp.bfloat16)
    head_grads = jnp.einsum('sktc,kdc->sktd', field_grad.astype(jnp.float32), head_w, precision=highest)
    pick_f = layer_pick.astype(jnp.float32)[:, :, None, None]
    grad_out = lax.optimization_barrier(jnp.sum(pick_f * head_grads, 1))
    grad_embed = lax.optimization_barrier(jnp.sum((1.0 - pick_f) * head_grads, 1))
    hidden_grad = jnp.einsum('std,fd->stf', grad_out.astype(jnp.bfloat16).astype(jnp.float32), down_weight.astype(jnp.float32), precision=highest)
    preact_grad = (hidden_grad * gelu_slope(preact)).astype(jnp.bfloat16)
    input_grad = jnp.einsum('stf,df->std', preact_grad.astype(jnp.float32), up_weight.astype(jnp.float32), precision=highest)
    scaled = input_grad * mod_gain
    mean_one = lax.optimization_barrier(jnp.mean(scaled, -1, keepdims=True))
    mean_two = lax.optimization_barrier(jnp.mean(scaled * centered, -1, keepdims=True))
    embed_grad = (scaled - mean_one - centered * mean_two) * inv_std + grad_out + grad_embed
    latent_part = jnp.einsum('std,cd->stc', embed_grad.astype(jnp.bfloat16).astype(jnp.float32), teacher_embed.astype(jnp.float32), precision=highest)
    latent_grad = retain * latent_part
    return (latents, logits, latent_grad)
```

```python
import math

import jax
import jax.numpy as jnp
from jax import lax
from jax.sharding import PartitionSpec as P

GRID_W = 64


EPSILON = 1e-06
GELU_COEF = 0.7978845608028654


def gelu_tanh(values):
    inner = GELU_COEF * (values + 0.044715 * values * values * values)
    return 0.5 * values * (1.0 + jnp.tanh(inner))


def gelu_slope(values):
    inner = GELU_COEF * (values + 0.044715 * values * values * values)
    tangent = jnp.tanh(inner)
    return 0.5 * (1.0 + tangent) + 0.5 * values * (1.0 - tangent * tangent) * GELU_COEF * (
        1.0 + 3.0 * 0.044715 * values * values
    )


def time_features(timestep, width):
    half_width = width // 2
    index = jnp.arange(half_width, dtype=jnp.float32)
    freqs = jnp.exp(-math.log(10000.0) * index / half_width)
    angles = timestep.astype(jnp.float32)[:, None] * freqs[None, :]
    return jnp.concatenate([jnp.cos(angles), jnp.sin(angles)], axis=-1)


def shifted(grid, offset):
    zero = jnp.zeros_like(grid[:, :, :1])
    if offset == -1:
        return jnp.concatenate([zero, grid[:, :, :-1]], axis=2)
    if offset == 1:
        return jnp.concatenate([grid[:, :, 1:], zero], axis=2)
    return grid


def conv_rows(grid, kernel, sign):
    rows = grid.shape[1] - 2
    total = None
    moved = {off: shifted(grid, off) for off in (-1, 0, 1)}
    for i in range(3):
        for j in range(3):
            row = 1 + sign * (i - 1)
            term = kernel[:, i, j][:, None, None, :] * moved[sign * (j - 1)][:, row : row + rows]
            total = term if total is None else total + term
    return total


def per_device(
    student_hidden,
    student_cond,
    student_mod,
    student_out,
    timestep,
    noise,
    teacher_embed,
    teacher_mod,
    up_weight,
    down_weight,
    head_proj,
    head_kernel,
    head_out,
    disc_layer,
):
    highest = lax.Precision.HIGHEST
    f32, bf16 = jnp.float32, jnp.bfloat16
    n_mp, n_seq = lax.axis_size("mp"), lax.axis_size("seq")
    seq = lax.axis_index("seq")
    tokens = student_hidden.shape[1]
    rows = tokens // GRID_W
    local_width = student_hidden.shape[2]
    width = local_width * n_mp
    latent_width = noise.shape[2]
    heads, _, channels = head_proj.shape
    picked = heads // 2

    reads = (disc_layer[0] == 1).astype(jnp.int32)
    order = jnp.arange(heads)
    rank = jnp.sum(jnp.where(order[None, :] < order[:, None], reads[None, :], 0), axis=1)
    slot_head = [
        jnp.sum(jnp.where((reads == 1) & (rank == j), jnp.arange(heads), 0)) for j in range(picked)
    ]
    one_hot = jnp.stack(
        [((reads == 1) & (rank == j)).astype(f32) for j in range(picked)], axis=1
    )

    embed_full = lax.all_gather(teacher_embed, "mp", axis=1, tiled=True)
    tmod = jnp.einsum(
        "f,fjd->jd",
        time_features(timestep, teacher_mod.shape[0])[0],
        teacher_mod.astype(f32),
        precision=highest,
    )
    tmod = lax.all_gather(tmod, "mp", axis=1, tiled=True)
    chunk = width // n_seq
    start = seq * chunk
    owner = start // local_width
    offset = start - owner * local_width
    own_proj = jnp.stack(
        [
            lax.dynamic_slice(head_proj, (slot_head[j], offset, 0), (1, chunk, channels))[0]
            for j in range(picked)
        ],
        axis=1,
    ).reshape(chunk, picked * channels)
    own_proj = jnp.where(lax.axis_index("mp") == owner, own_proj, jnp.zeros_like(own_proj))
    proj_chunk = lax.psum(own_proj, "mp")
    out_fold = lax.psum(
        jnp.dot(down_weight, proj_chunk, preferred_element_type=f32).astype(bf16), "seq"
    )
    embed_f = embed_full.astype(f32)
    embed_centered = embed_f - jnp.mean(embed_f, axis=1, keepdims=True)
    gram = jnp.einsum("cd,ed->ce", embed_centered, embed_centered, precision=highest)
    stacked = jnp.concatenate(
        [embed_centered * (1.0 + tmod[1:2]), tmod[0:1]], axis=0
    ).astype(bf16)
    stacked = lax.dynamic_slice_in_dim(stacked, start, chunk, 1)
    in_fold = lax.psum(
        jnp.dot(stacked, up_weight, preferred_element_type=f32).astype(bf16), "seq"
    )
    embed_proj = lax.psum(
        jnp.einsum("cd,kdh->kch", teacher_embed, head_proj, preferred_element_type=f32), "mp"
    )

    hidden = student_hidden[0].astype(f32)
    first_sum, square_sum = lax.psum((jnp.sum(hidden, -1), jnp.sum(hidden * hidden, -1)), "mp")
    tok_mean = (first_sum / width)[:, None]
    tok_var = (square_sum / width)[:, None] - tok_mean * tok_mean
    half_mod = jnp.einsum(
        "sk,kjd->sjd", student_cond, student_mod.astype(f32), precision=highest
    )
    half_mod = lax.psum(half_mod, "seq")
    halves_all = lax.all_gather(half_mod, "group", axis=1, tiled=True)
    own_mod = lax.dynamic_slice_in_dim(halves_all, lax.axis_index("group"), 1, 0)[0]
    normed = (
        (hidden - tok_mean) * lax.rsqrt(tok_var + EPSILON) * (1.0 + own_mod[1:2]) + own_mod[0:1]
    ).astype(bf16)
    latents = lax.psum(
        jnp.dot(normed, student_out, preferred_element_type=f32).astype(bf16), "mp"
    )
    level = timestep[0].astype(f32) / 1000.0
    retain = 1.0 - level
    noised = (retain * latents.astype(f32) + level * noise[0].astype(f32)).astype(bf16)

    halo = 2 * GRID_W
    ups = [(i, i + 1) for i in range(n_seq - 1)]
    downs = [(j, i) for i, j in ups]
    before = lax.ppermute(noised[tokens - halo :], "seq", ups)
    after = lax.ppermute(noised[:halo], "seq", downs)
    wide = jnp.concatenate([before, noised, after], axis=0)

    wide_f = wide.astype(f32)
    wide_gram = jnp.dot(wide_f, gram, precision=highest)
    var_t = jnp.sum(wide_f * wide_gram, -1, keepdims=True) / width
    inv_std = lax.rsqrt(var_t + EPSILON)
    up_fold = in_fold[:latent_width]
    bias = in_fold[latent_width:].astype(f32)
    preact = inv_std * jnp.dot(wide, up_fold, preferred_element_type=f32) + bias
    activated = gelu_tanh(preact).astype(bf16)
    block_terms = lax.psum(
        jnp.dot(activated, out_fold, preferred_element_type=f32).astype(bf16), "mp"
    ).astype(f32)
    projected = jnp.einsum("tc,kch->kth", wide_f, embed_proj, precision=highest)
    projected = projected + sum(
        one_hot[:, j][:, None, None]
        * block_terms[:, j * channels : (j + 1) * channels][None]
        for j in range(picked)
    )
    grid = projected.reshape(heads, rows + 4, GRID_W, channels)
    row_id = seq * rows - 2 + jnp.arange(rows + 4)
    inside = ((row_id >= 0) & (row_id < rows * n_seq)).astype(f32)[None, :, None, None]
    conv_field = conv_rows(grid * inside, head_kernel, 1)
    gating = jax.nn.sigmoid(conv_field)
    out_scale = head_out[:, None, None, :]
    logits = jnp.sum((conv_field * gating * out_scale)[:, 1 : rows + 1], -1).reshape(
        1, heads, tokens
    )
    slope_grad = -out_scale * gating * (1.0 + conv_field * (1.0 - gating)) * inside[:, 1:-1]
    field_grad = conv_rows(slope_grad, head_kernel, -1).reshape(heads, tokens, channels)
    field_grad = field_grad.astype(bf16)
    head_part = jnp.einsum("kth,kch->tc", field_grad.astype(f32), embed_proj, precision=highest)
    picked_grad = jnp.concatenate(
        [
            jnp.sum(field_grad * one_hot[:, j][:, None, None].astype(bf16), 0)
            for j in range(picked)
        ],
        axis=1,
    )
    hidden_grad = lax.dot_general(
        picked_grad, out_fold, (((1,), (1,)), ((), ())), preferred_element_type=f32
    )
    own = slice(halo, halo + tokens)
    preact_grad = (hidden_grad * gelu_slope(preact[own])).astype(bf16)
    scaled_back = lax.psum(
        lax.dot_general(
            preact_grad, up_fold, (((1,), (1,)), ((), ())), preferred_element_type=f32
        ),
        "mp",
    )
    noised_f, own_inv = wide_f[own], inv_std[own]
    along = jnp.sum(noised_f * scaled_back, -1, keepdims=True) / width
    latent_grad = retain * (
        (scaled_back - own_inv * own_inv * wide_gram[own] * along) * own_inv + head_part
    )
    return (latents[None], logits, latent_grad[None])


def solution(mesh):
    return jax.shard_map(
        per_device,
        mesh=mesh,
        in_specs=(
            P("group", "seq", "mp"),
            P(None, "seq"),
            P("seq", "group", "mp"),
            P("mp", None),
            P("group"),
            P("group", "seq", None),
            P(None, "mp"),
            P(None, None, "mp"),
            P("seq", "mp"),
            P("mp", "seq"),
            P(None, "mp", None),
            P(),
            P(),
            P("group", None),
        ),
        out_specs=(P("group", "seq", None), P("group", None, "seq"), P("group", "seq", None)),
        check_vma=False,
    )
```

```python
import functools
import math

import jax
import jax.numpy as jnp
from jax import lax
from jax.experimental import pallas as pl
from jax.experimental.pallas import tpu as pltpu
from jax.sharding import PartitionSpec as P

GRID_W = 64


EPSILON = 1e-06
GELU_COEF = 0.7978845608028654


def gelu_tanh(values):
    inner = GELU_COEF * (values + 0.044715 * values * values * values)
    return 0.5 * values * (1.0 + jnp.tanh(inner))


def gelu_slope(values):
    inner = GELU_COEF * (values + 0.044715 * values * values * values)
    tangent = jnp.tanh(inner)
    return 0.5 * (1.0 + tangent) + 0.5 * values * (1.0 - tangent * tangent) * GELU_COEF * (
        1.0 + 3.0 * 0.044715 * values * values
    )


def time_features(timestep, width):
    half_width = width // 2
    index = jnp.arange(half_width, dtype=jnp.float32)
    freqs = jnp.exp(-math.log(10000.0) * index / half_width)
    angles = timestep.astype(jnp.float32)[:, None] * freqs[None, :]
    return jnp.concatenate([jnp.cos(angles), jnp.sin(angles)], axis=-1)


MESH = pl.DeviceIdType.MESH
NEAR = 2
PIECES = 4


def fold_kernel(
    n_group, n_seq, pieces, fold_ref, mod_ref, out_ref, mod_out_ref,
    near_in, part, far_in, mod_in, near_sems, far_sems, back_sems, last_sems, mod_sems,
):
    far = n_seq // NEAR
    group, seq = lax.axis_index("group"), lax.axis_index("seq")
    my_far, my_near = seq // NEAR, lax.rem(seq, NEAR)
    other = lax.rem(my_near + 1, NEAR)
    piece = fold_ref.shape[2] // pieces
    f32 = jnp.float32

    partners = [(dg, ds) for dg in range(n_group) for ds in range(n_seq) if dg or ds]
    barrier = pltpu.get_barrier_semaphore()
    for dg, ds in partners:
        target = {"group": lax.rem(group + dg, n_group), "seq": lax.rem(seq + ds, n_seq)}
        pl.semaphore_signal(barrier, inc=1, device_id=target, device_id_type=MESH)
    pl.semaphore_wait(barrier, len(partners))

    def far_id(step):
        return lax.rem(my_far + step, far) * NEAR + my_near

    def rows(s):
        return pl.ds(s * piece, piece)

    mod_copies = []
    for dg, ds in partners:
        to_group = lax.rem(group + dg, n_group)
        copy = pltpu.make_async_remote_copy(
            src_ref=mod_ref.at[to_group],
            dst_ref=mod_in.at[dg, ds],
            send_sem=mod_sems.at[0, dg, ds],
            recv_sem=mod_sems.at[1, dg, ds],
            device_id={"group": to_group, "seq": lax.rem(seq + ds, n_seq)},
            device_id_type=MESH,
        )
        copy.start()
        mod_copies.append(copy)
    near_copies = []
    for s in range(pieces):
        copy = pltpu.make_async_remote_copy(
            src_ref=fold_ref.at[other, :, rows(s)],
            dst_ref=near_in.at[:, rows(s)],
            send_sem=near_sems.at[0, s],
            recv_sem=near_sems.at[1, s],
            device_id={"seq": my_far * NEAR + other},
            device_id_type=MESH,
        )
        copy.start()
        near_copies.append(copy)
    mod_in[0, 0] = mod_ref[group]

    far_copies, back_copies, last_copies = {}, {}, {}
    for s in range(pieces):
        near_copies[s].wait_recv()
        part[:, rows(s)] = (
            fold_ref[my_near, :, rows(s)].astype(f32) + near_in[:, rows(s)].astype(f32)
        ).astype(part.dtype)
        for k in range(1, far):
            copy = pltpu.make_async_remote_copy(
                src_ref=part.at[lax.rem(my_far + k, far), rows(s)],
                dst_ref=far_in.at[k - 1, rows(s)],
                send_sem=far_sems.at[0, s, k - 1],
                recv_sem=far_sems.at[1, s, k - 1],
                device_id={"seq": far_id(k)},
                device_id_type=MESH,
            )
            copy.start()
            far_copies[s, k] = copy

    def finish(s):
        for k in range(1, far):
            back_copies[s, k].wait_recv()
        copy = pltpu.make_async_remote_copy(
            src_ref=out_ref.at[my_near, :, rows(s)],
            dst_ref=out_ref.at[my_near, :, rows(s)],
            send_sem=last_sems.at[0, s],
            recv_sem=last_sems.at[1, s],
            device_id={"seq": my_far * NEAR + other},
            device_id_type=MESH,
        )
        copy.start()
        last_copies[s] = copy

    for s in range(pieces):
        total = part[my_far, rows(s)].astype(f32)
        for k in range(1, far):
            far_copies[s, k].wait_recv()
            total = total + far_in[k - 1, rows(s)].astype(f32)
        out_ref[my_near, my_far, rows(s)] = total.astype(out_ref.dtype)
        for k in range(1, far):
            copy = pltpu.make_async_remote_copy(
                src_ref=out_ref.at[my_near, my_far, rows(s)],
                dst_ref=out_ref.at[my_near, my_far, rows(s)],
                send_sem=back_sems.at[0, s, k - 1],
                recv_sem=back_sems.at[1, s, k - 1],
                device_id={"seq": far_id(k)},
                device_id_type=MESH,
            )
            copy.start()
            back_copies[s, k] = copy
        if s >= 1:
            finish(s - 1)
    for copy in mod_copies:
        copy.wait_recv()
    for dg in range(n_group):
        total = mod_in[dg, 0]
        for ds in range(1, n_seq):
            total = total + mod_in[dg, ds]
        mod_out_ref[lax.rem(group + n_group - dg, n_group)] = total
    finish(pieces - 1)
    for s in range(pieces):
        last_copies[s].wait_recv()
    for copies in (mod_copies, near_copies, far_copies.values(), back_copies.values(), last_copies.values()):
        for copy in copies:
            copy.wait_send()


def summed_folds(fold, mod, n_group, n_seq):
    hidden, lanes = fold.shape
    share = hidden // n_seq
    far = n_seq // NEAR
    mod_rows = mod.shape[1] // 128
    fits = hidden % n_seq == 0 and n_seq % NEAR == 0 and far > 1 and share % (16 * PIECES) == 0
    if not fits or mod.shape[1] % 128 or mod.shape[0] != n_group:
        halves = lax.all_gather(lax.psum(mod, "seq"), "group", axis=1)
        own = lax.dynamic_slice_in_dim(halves, lax.axis_index("group"), 1, 0)[0]
        return lax.psum(fold, "seq"), own
    dma = pltpu.SemaphoreType.DMA
    summed, own = pl.pallas_call(
        functools.partial(fold_kernel, n_group, n_seq, PIECES),
        out_shape=(
            jax.ShapeDtypeStruct((NEAR, far, share, lanes), fold.dtype),
            jax.ShapeDtypeStruct((n_group, mod_rows, 128), jnp.float32),
        ),
        in_specs=[pl.BlockSpec(memory_space=pltpu.VMEM)] * 2,
        out_specs=(pl.BlockSpec(memory_space=pltpu.VMEM),) * 2,
        scratch_shapes=[
            pltpu.VMEM((far, share, lanes), fold.dtype),
            pltpu.VMEM((far, share, lanes), fold.dtype),
            pltpu.VMEM((far - 1, share, lanes), fold.dtype),
            pltpu.VMEM((n_group, n_seq, mod_rows, 128), jnp.float32),
            dma((2, PIECES)),
            dma((2, PIECES, far - 1)),
            dma((2, PIECES, far - 1)),
            dma((2, PIECES)),
            dma((2, n_group, n_seq)),
        ],
        compiler_params=pltpu.CompilerParams(
            collective_id=0, has_side_effects=True, vmem_limit_bytes=40 * 1024 * 1024
        ),
    )(fold.reshape(NEAR, far, share, lanes), mod.reshape(mod.shape[0], mod_rows, 128))
    return summed.reshape(hidden, lanes), own.reshape(n_group, mod.shape[1])


def shifted(grid, offset):
    zero = jnp.zeros_like(grid[:, :, :1])
    if offset == -1:
        return jnp.concatenate([zero, grid[:, :, :-1]], axis=2)
    if offset == 1:
        return jnp.concatenate([grid[:, :, 1:], zero], axis=2)
    return grid


def conv_rows(grid, kernel, sign):
    rows = grid.shape[1] - 2
    total = None
    moved = {off: shifted(grid, off) for off in (-1, 0, 1)}
    for i in range(3):
        for j in range(3):
            row = 1 + sign * (i - 1)
            term = kernel[:, i, j][:, None, None, :] * moved[sign * (j - 1)][:, row : row + rows]
            total = term if total is None else total + term
    return total


def per_device(
    student_hidden,
    student_cond,
    student_mod,
    student_out,
    timestep,
    noise,
    teacher_embed,
    teacher_mod,
    up_weight,
    down_weight,
    head_proj,
    head_kernel,
    head_out,
    disc_layer,
):
    highest = lax.Precision.HIGHEST
    f32, bf16 = jnp.float32, jnp.bfloat16
    n_mp, n_seq = lax.axis_size("mp"), lax.axis_size("seq")
    seq = lax.axis_index("seq")
    tokens = student_hidden.shape[1]
    rows = tokens // GRID_W
    local_width = student_hidden.shape[2]
    width = local_width * n_mp
    latent_width = noise.shape[2]
    heads, _, channels = head_proj.shape
    picked = heads // 2

    reads = (disc_layer[0] == 1).astype(jnp.int32)
    order = jnp.arange(heads)
    rank = jnp.sum(jnp.where(order[None, :] < order[:, None], reads[None, :], 0), axis=1)
    slot_head = [
        jnp.sum(jnp.where((reads == 1) & (rank == j), jnp.arange(heads), 0)) for j in range(picked)
    ]
    one_hot = jnp.stack(
        [((reads == 1) & (rank == j)).astype(f32) for j in range(picked)], axis=1
    )

    embed_full = lax.all_gather(teacher_embed, "mp", axis=1, tiled=True)
    tmod = jnp.einsum(
        "f,fjd->jd",
        time_features(timestep, teacher_mod.shape[0])[0],
        teacher_mod.astype(f32),
        precision=highest,
    )
    tmod = lax.all_gather(tmod, "mp", axis=1, tiled=True)
    chunk = width // n_seq
    start = seq * chunk
    owner = start // local_width
    offset = start - owner * local_width
    own_proj = jnp.stack(
        [
            lax.dynamic_slice(head_proj, (slot_head[j], offset, 0), (1, chunk, channels))[0]
            for j in range(picked)
        ],
        axis=1,
    ).reshape(chunk, picked * channels)
    own_proj = lax.all_gather(own_proj, "mp")
    proj_chunk = lax.dynamic_index_in_dim(own_proj, owner, 0, keepdims=False)
    out_terms = jnp.dot(down_weight, proj_chunk, preferred_element_type=f32).astype(bf16)
    embed_f = embed_full.astype(f32)
    embed_centered = embed_f - jnp.mean(embed_f, axis=1, keepdims=True)
    gram = jnp.einsum("cd,ed->ce", embed_centered, embed_centered, precision=highest)
    stacked = jnp.concatenate(
        [embed_centered * (1.0 + tmod[1:2]), tmod[0:1]], axis=0
    ).astype(bf16)
    stacked = lax.dynamic_slice_in_dim(stacked, start, chunk, 1)
    pad = -stacked.shape[0] % 128
    stacked = jnp.pad(stacked, ((0, pad), (0, 0)))
    in_terms = lax.dot_general(
        up_weight, stacked, (((0,), (1,)), ((), ())), preferred_element_type=f32
    ).astype(bf16)
    embed_proj = jnp.einsum("cd,kdh->kch", teacher_embed, head_proj, preferred_element_type=f32)
    embed_proj = jnp.sum(lax.all_gather(embed_proj, "mp"), axis=0)

    hidden = student_hidden[0].astype(f32)
    first_sum, square_sum = lax.psum((jnp.sum(hidden, -1), jnp.sum(hidden * hidden, -1)), "mp")
    tok_mean = (first_sum / width)[:, None]
    tok_var = (square_sum / width)[:, None] - tok_mean * tok_mean
    half_mod = jnp.einsum(
        "sk,kjd->sjd", student_cond, student_mod.astype(f32), precision=highest
    )
    folds, own_mod = summed_folds(
        jnp.concatenate([out_terms, in_terms], axis=1),
        half_mod[:, 0],
        lax.axis_size("group"),
        n_seq,
    )
    out_fold = folds[:, : picked * channels]
    up_fold = folds[:, picked * channels : picked * channels + latent_width]
    bias = folds[:, picked * channels + latent_width].astype(f32)[None]
    normed = (
        (hidden - tok_mean) * lax.rsqrt(tok_var + EPSILON) * (1.0 + own_mod[1:2]) + own_mod[0:1]
    ).astype(bf16)
    latents = lax.psum(
        jnp.dot(normed, student_out, preferred_element_type=f32).astype(bf16), "mp"
    )
    level = timestep[0].astype(f32) / 1000.0
    retain = 1.0 - level
    noised = (retain * latents.astype(f32) + level * noise[0].astype(f32)).astype(bf16)

    halo = 2 * GRID_W
    ups = [(i, i + 1) for i in range(n_seq - 1)]
    downs = [(j, i) for i, j in ups]
    before = lax.ppermute(noised[tokens - halo :], "seq", ups)
    after = lax.ppermute(noised[:halo], "seq", downs)
    wide = jnp.concatenate([before, noised, after], axis=0)

    wide_f = wide.astype(f32)
    wide_gram = jnp.dot(wide_f, gram, precision=highest)
    var_t = jnp.sum(wide_f * wide_gram, -1, keepdims=True) / width
    inv_std = lax.rsqrt(var_t + EPSILON)
    preact = (
        inv_std
        * lax.dot_general(wide, up_fold, (((1,), (1,)), ((), ())), preferred_element_type=f32)
        + bias
    )
    activated = gelu_tanh(preact).astype(bf16)
    block_terms = jnp.dot(activated, out_fold, preferred_element_type=f32).astype(bf16)
    block_terms = jnp.sum(lax.all_gather(block_terms, "mp").astype(f32), axis=0)
    projected = jnp.einsum("tc,kch->kth", wide_f, embed_proj, precision=highest)
    projected = projected + sum(
        one_hot[:, j][:, None, None]
        * block_terms[:, j * channels : (j + 1) * channels][None]
        for j in range(picked)
    )
    grid = projected.reshape(heads, rows + 4, GRID_W, channels)
    row_id = seq * rows - 2 + jnp.arange(rows + 4)
    inside = ((row_id >= 0) & (row_id < rows * n_seq)).astype(f32)[None, :, None, None]
    conv_field = conv_rows(grid * inside, head_kernel, 1)
    gating = jax.nn.sigmoid(conv_field)
    out_scale = head_out[:, None, None, :]
    logits = jnp.sum((conv_field * gating * out_scale)[:, 1 : rows + 1], -1).reshape(
        1, heads, tokens
    )
    slope_grad = -out_scale * gating * (1.0 + conv_field * (1.0 - gating)) * inside[:, 1:-1]
    field_grad = conv_rows(slope_grad, head_kernel, -1).reshape(heads, tokens, channels)
    field_grad = field_grad.astype(bf16)
    head_part = jnp.einsum("kth,kch->tc", field_grad.astype(f32), embed_proj, precision=highest)
    picked_grad = jnp.concatenate(
        [
            jnp.sum(field_grad * one_hot[:, j][:, None, None].astype(bf16), 0)
            for j in range(picked)
        ],
        axis=1,
    )
    hidden_grad = lax.dot_general(
        picked_grad, out_fold, (((1,), (1,)), ((), ())), preferred_element_type=f32
    )
    own = slice(halo, halo + tokens)
    preact_grad = (hidden_grad * gelu_slope(preact[own])).astype(bf16)
    scaled_back = lax.psum(
        jnp.dot(preact_grad, up_fold, preferred_element_type=f32),
        "mp",
    )
    noised_f, own_inv = wide_f[own], inv_std[own]
    along = jnp.sum(noised_f * scaled_back, -1, keepdims=True) / width
    latent_grad = retain * (
        (scaled_back - own_inv * own_inv * wide_gram[own] * along) * own_inv + head_part
    )
    return (latents[None], logits, latent_grad[None])


def solution(mesh):
    return jax.shard_map(
        per_device,
        mesh=mesh,
        in_specs=(
            P("group", "seq", "mp"),
            P(None, "seq"),
            P("seq", "group", "mp"),
            P("mp", None),
            P("group"),
            P("group", "seq", None),
            P(None, "mp"),
            P(None, None, "mp"),
            P("seq", "mp"),
            P("mp", "seq"),
            P(None, "mp", None),
            P(),
            P(),
            P("group", None),
        ),
        out_specs=(P("group", "seq", None), P("group", None, "seq"), P("group", "seq", None)),
        check_vma=False,
    )
```

```python
import functools
import math

import jax
import jax.numpy as jnp
from jax import lax
from jax.experimental import pallas as pl
from jax.experimental.pallas import tpu as pltpu
from jax.sharding import PartitionSpec as P

GRID_W = 64


EPSILON = 1e-06
GELU_COEF = 0.7978845608028654


def gelu_tanh(values):
    inner = GELU_COEF * (values + 0.044715 * values * values * values)
    return 0.5 * values * (1.0 + jnp.tanh(inner))


def gelu_slope(values):
    inner = GELU_COEF * (values + 0.044715 * values * values * values)
    tangent = jnp.tanh(inner)
    return 0.5 * (1.0 + tangent) + 0.5 * values * (1.0 - tangent * tangent) * GELU_COEF * (
        1.0 + 3.0 * 0.044715 * values * values
    )


def time_features(timestep, width):
    half_width = width // 2
    index = jnp.arange(half_width, dtype=jnp.float32)
    freqs = jnp.exp(-math.log(10000.0) * index / half_width)
    angles = timestep.astype(jnp.float32)[:, None] * freqs[None, :]
    return jnp.concatenate([jnp.cos(angles), jnp.sin(angles)], axis=-1)


MESH = pl.DeviceIdType.MESH
NEAR = 2
PIECES = 4


def fold_kernel(n_group, n_seq, n_mp, pieces, fold_ref, slim_ref, mod_ref, *refs):
    fold_out, slim_out, mod_out_ref = refs[2:5]
    pair_refs, pair_outs = refs[:2], refs[5:7]
    (
        near_in, part, far_in, slim_near, slim_part, slim_far, mod_in, *pair_in,
        near_sems, far_sems, back_sems, last_sems, mod_sems, pair_sems,
    ) = refs[7:]
    far = n_seq // NEAR
    group, seq, mp = lax.axis_index("group"), lax.axis_index("seq"), lax.axis_index("mp")
    my_far, my_near = seq // NEAR, lax.rem(seq, NEAR)
    other = lax.rem(my_near + 1, NEAR)
    piece = fold_ref.shape[2] // pieces
    share = fold_ref.shape[2]
    half = far * share
    f32 = jnp.float32

    partners = [(dg, ds) for dg in range(n_group) for ds in range(n_seq) if dg or ds]
    barrier = pltpu.get_barrier_semaphore()
    for dg, ds in partners:
        target = {"group": lax.rem(group + dg, n_group), "seq": lax.rem(seq + ds, n_seq)}
        pl.semaphore_signal(barrier, inc=1, device_id=target, device_id_type=MESH)
    for dm in range(1, n_mp):
        target = {"mp": lax.rem(mp + dm, n_mp)}
        pl.semaphore_signal(barrier, inc=1, device_id=target, device_id_type=MESH)
    pl.semaphore_wait(barrier, len(partners) + n_mp - 1)

    def far_id(step):
        return lax.rem(my_far + step, far) * NEAR + my_near

    def lanes(start, size):
        return pl.ds(pl.multiple_of(start, 128), size)

    def rows(s):
        return pl.ds((s - 1) * piece, piece)

    def source(s, near):
        return slim_ref.at[:, lanes(near * half, half)] if s == 0 else fold_ref.at[near, :, rows(s)]

    def from_near(s):
        return slim_near if s == 0 else near_in.at[:, rows(s)]

    def partial(s):
        return slim_part if s == 0 else part.at[:, rows(s)]

    def partial_of(s, z):
        return slim_part.at[:, lanes(z * share, share)] if s == 0 else part.at[z, rows(s)]

    def from_far(s, k):
        return slim_far.at[k - 1] if s == 0 else far_in.at[k - 1, rows(s)]

    def result_of(s):
        if s == 0:
            return slim_out.at[:, lanes(my_near * half + my_far * share, share)]
        return fold_out.at[my_near, my_far, rows(s)]

    def result(s):
        if s == 0:
            return slim_out.at[:, lanes(my_near * half, half)]
        return fold_out.at[my_near, :, rows(s)]

    def send(src, dst, sems, index, target):
        copy = pltpu.make_async_remote_copy(
            src_ref=src,
            dst_ref=dst,
            send_sem=sems.at[(0, *index)],
            recv_sem=sems.at[(1, *index)],
            device_id=target,
            device_id_type=MESH,
        )
        copy.start()
        return copy

    count = pieces + 1
    across = {"seq": my_far * NEAR + other}
    near_copies = [
        send(source(s, other), from_near(s), near_sems, (s,), across) for s in range(count)
    ]
    mod_copies = []
    for dg, ds in partners:
        to_group = lax.rem(group + dg, n_group)
        target = {"group": to_group, "seq": lax.rem(seq + ds, n_seq)}
        mod_copies.append(
            send(mod_ref.at[to_group], mod_in.at[dg, ds], mod_sems, (dg, ds), target)
        )
    pair_copies = [
        send(pair_refs[i], pair_in[i].at[dm], pair_sems, (i, dm), {"mp": lax.rem(mp + dm, n_mp)})
        for i in range(2)
        for dm in range(1, n_mp)
    ]

    far_copies, back_copies, last_copies = {}, {}, {}
    for s in range(count):
        near_copies[s].wait_recv()
        partial(s)[...] = (
            source(s, my_near)[...].astype(f32) + from_near(s)[...].astype(f32)
        ).astype(part.dtype)
        for k in range(1, far):
            far_copies[s, k] = send(
                partial_of(s, lax.rem(my_far + k, far)),
                from_far(s, k),
                far_sems,
                (s, k - 1),
                {"seq": far_id(k)},
            )

    def finish(s):
        for k in range(1, far):
            back_copies[s, k].wait_recv()
        last_copies[s] = send(result(s), result(s), last_sems, (s,), across)

    for s in range(count):
        total = partial_of(s, my_far)[...].astype(f32)
        for k in range(1, far):
            far_copies[s, k].wait_recv()
            total = total + from_far(s, k)[...].astype(f32)
        result_of(s)[...] = total.astype(fold_out.dtype)
        for k in range(1, far):
            back_copies[s, k] = send(
                result_of(s), result_of(s), back_sems, (s, k - 1), {"seq": far_id(k)}
            )
        if s >= 1:
            finish(s - 1)
    for copy in mod_copies + pair_copies:
        copy.wait_recv()
    for dg in range(n_group):
        total = mod_ref[group] if dg == 0 else mod_in[dg, 0]
        for ds in range(1, n_seq):
            total = total + mod_in[dg, ds]
        mod_out_ref[lax.rem(group + n_group - dg, n_group)] = total
    for i in range(2):
        total = pair_refs[i][...]
        for dm in range(1, n_mp):
            total = total + pair_in[i][dm]
        pair_outs[i][...] = total
    finish(pieces)
    for s in range(count):
        last_copies[s].wait_recv()
    for copies in (near_copies, far_copies.values(), back_copies.values(), last_copies.values()):
        for copy in copies:
            copy.wait_send()
    for copy in mod_copies + pair_copies:
        copy.wait_send()


def summed_folds(fold, slim, mod, pair):
    n_group, n_seq, n_mp = (lax.axis_size(axis) for axis in ("group", "seq", "mp"))
    hidden, columns = fold.shape
    share = hidden // n_seq
    far = n_seq // NEAR
    mod_rows = mod.shape[1] // 128
    fits = hidden % n_seq == 0 and n_seq % NEAR == 0 and far > 1 and share % (16 * PIECES) == 0
    if not fits or share % 128 or mod.shape[1] % 128 or mod.shape[0] != n_group:
        halves = lax.all_gather(lax.psum(mod, "seq"), "group", axis=1)
        own = lax.dynamic_slice_in_dim(halves, lax.axis_index("group"), 1, 0)[0]
        return lax.psum(fold, "seq"), lax.psum(slim, "seq"), own, lax.psum(pair, "mp")
    dma = pltpu.SemaphoreType.DMA
    vmem = pl.BlockSpec(memory_space=pltpu.VMEM)
    tall, kind, height = PIECES + 1, fold.dtype, slim.shape[0]
    summed, slim_sum, own, *pair_sum = pl.pallas_call(
        functools.partial(fold_kernel, n_group, n_seq, n_mp, PIECES),
        out_shape=(
            jax.ShapeDtypeStruct((NEAR, far, share, columns), kind),
            jax.ShapeDtypeStruct(slim.shape, kind),
            jax.ShapeDtypeStruct((n_group, mod_rows, 128), jnp.float32),
            *(jax.ShapeDtypeStruct(value.shape, value.dtype) for value in pair),
        ),
        in_specs=[vmem] * 5,
        out_specs=(vmem,) * 5,
        scratch_shapes=[
            pltpu.VMEM((far, share, columns), kind),
            pltpu.VMEM((far, share, columns), kind),
            pltpu.VMEM((far - 1, share, columns), kind),
            pltpu.VMEM((height, far * share), kind),
            pltpu.VMEM((height, far * share), kind),
            pltpu.VMEM((far - 1, height, share), kind),
            pltpu.VMEM((n_group, n_seq, mod_rows, 128), jnp.float32),
            *(pltpu.VMEM((n_mp, *value.shape), value.dtype) for value in pair),
            dma((2, tall)),
            dma((2, tall, far - 1)),
            dma((2, tall, far - 1)),
            dma((2, tall)),
            dma((2, n_group, n_seq)),
            dma((2, 2, n_mp)),
        ],
        compiler_params=pltpu.CompilerParams(
            collective_id=0, has_side_effects=True, vmem_limit_bytes=40 * 1024 * 1024
        ),
    )(
        fold.reshape(NEAR, far, share, columns),
        slim,
        mod.reshape(mod.shape[0], mod_rows, 128),
        *pair,
    )
    return summed.reshape(hidden, columns), slim_sum, own.reshape(n_group, mod.shape[1]), pair_sum


def shifted(grid, offset):
    zero = jnp.zeros_like(grid[:, :, :1])
    if offset == -1:
        return jnp.concatenate([zero, grid[:, :, :-1]], axis=2)
    if offset == 1:
        return jnp.concatenate([grid[:, :, 1:], zero], axis=2)
    return grid


def conv_rows(grid, kernel, sign):
    rows = grid.shape[1] - 2
    total = None
    moved = {off: shifted(grid, off) for off in (-1, 0, 1)}
    for i in range(3):
        for j in range(3):
            row = 1 + sign * (i - 1)
            term = kernel[:, i, j][:, None, None, :] * moved[sign * (j - 1)][:, row : row + rows]
            total = term if total is None else total + term
    return total


def per_device(
    student_hidden,
    student_cond,
    student_mod,
    student_out,
    timestep,
    noise,
    teacher_embed,
    teacher_mod,
    up_weight,
    down_weight,
    head_proj,
    head_kernel,
    head_out,
    disc_layer,
):
    highest = lax.Precision.HIGHEST
    f32, bf16 = jnp.float32, jnp.bfloat16
    n_mp, n_seq = lax.axis_size("mp"), lax.axis_size("seq")
    seq = lax.axis_index("seq")
    tokens = student_hidden.shape[1]
    rows = tokens // GRID_W
    local_width = student_hidden.shape[2]
    width = local_width * n_mp
    latent_width = noise.shape[2]
    heads, _, channels = head_proj.shape
    picked = heads // 2

    reads = (disc_layer[0] == 1).astype(jnp.int32)
    order = jnp.arange(heads)
    rank = jnp.sum(jnp.where(order[None, :] < order[:, None], reads[None, :], 0), axis=1)
    slot_head = [
        jnp.sum(jnp.where((reads == 1) & (rank == j), jnp.arange(heads), 0)) for j in range(picked)
    ]
    one_hot = jnp.stack(
        [((reads == 1) & (rank == j)).astype(f32) for j in range(picked)], axis=1
    )

    embed_full = lax.all_gather(teacher_embed, "mp", axis=1, tiled=True)
    tmod = jnp.einsum(
        "f,fjd->jd",
        time_features(timestep, teacher_mod.shape[0])[0],
        teacher_mod.astype(f32),
        precision=highest,
    )
    tmod = lax.all_gather(tmod, "mp", axis=1, tiled=True)
    chunk = width // n_seq
    start = seq * chunk
    owner = start // local_width
    offset = start - owner * local_width
    own_proj = jnp.stack(
        [
            lax.dynamic_slice(head_proj, (slot_head[j], offset, 0), (1, chunk, channels))[0]
            for j in range(picked)
        ],
        axis=1,
    ).reshape(chunk, picked * channels)
    own_proj = lax.all_gather(own_proj, "mp")
    proj_chunk = lax.dynamic_index_in_dim(own_proj, owner, 0, keepdims=False)
    out_terms = jnp.dot(down_weight, proj_chunk, preferred_element_type=f32).astype(bf16)
    embed_f = embed_full.astype(f32)
    embed_centered = embed_f - jnp.mean(embed_f, axis=1, keepdims=True)
    gram = jnp.einsum("cd,ed->ce", embed_centered, embed_centered, precision=highest)
    stacked = jnp.concatenate(
        [embed_centered * (1.0 + tmod[1:2]), tmod[0:1]], axis=0
    ).astype(bf16)
    stacked = lax.dynamic_slice_in_dim(stacked, start, chunk, 1)
    pad = -stacked.shape[0] % 16
    stacked = jnp.pad(stacked, ((0, pad), (0, 0)))
    in_terms = jnp.dot(stacked, up_weight, preferred_element_type=f32).astype(bf16)
    embed_proj = jnp.einsum("cd,kdh->kch", teacher_embed, head_proj, preferred_element_type=f32)

    hidden = student_hidden[0].astype(f32)
    token_sums = jnp.stack([jnp.sum(hidden, -1), jnp.sum(hidden * hidden, -1)])
    half_mod = jnp.einsum(
        "sk,kjd->sjd", student_cond, student_mod.astype(f32), precision=highest
    )
    out_fold, in_fold, own_mod, (token_sums, embed_proj) = summed_folds(
        out_terms, in_terms, half_mod[:, 0], (token_sums, embed_proj)
    )
    up_fold = in_fold[:latent_width]
    bias = in_fold[latent_width : latent_width + 1].astype(f32)
    tok_mean = (token_sums[0] / width)[:, None]
    tok_var = (token_sums[1] / width)[:, None] - tok_mean * tok_mean
    normed = (
        (hidden - tok_mean) * lax.rsqrt(tok_var + EPSILON) * (1.0 + own_mod[1:2]) + own_mod[0:1]
    ).astype(bf16)
    latents = lax.psum(
        jnp.dot(normed, student_out, preferred_element_type=f32).astype(bf16), "mp"
    )
    level = timestep[0].astype(f32) / 1000.0
    retain = 1.0 - level
    noised = (retain * latents.astype(f32) + level * noise[0].astype(f32)).astype(bf16)

    halo = 2 * GRID_W
    ups = [(i, i + 1) for i in range(n_seq - 1)]
    downs = [(j, i) for i, j in ups]
    before = lax.ppermute(noised[tokens - halo :], "seq", ups)
    after = lax.ppermute(noised[:halo], "seq", downs)
    wide = jnp.concatenate([before, noised, after], axis=0)

    wide_f = wide.astype(f32)
    wide_gram = jnp.dot(wide_f, gram, precision=highest)
    var_t = jnp.sum(wide_f * wide_gram, -1, keepdims=True) / width
    inv_std = lax.rsqrt(var_t + EPSILON)
    preact = inv_std * jnp.dot(wide, up_fold, preferred_element_type=f32) + bias
    activated = gelu_tanh(preact).astype(bf16)
    block_terms = jnp.dot(activated, out_fold, preferred_element_type=f32).astype(bf16)
    block_terms = jnp.sum(lax.all_gather(block_terms, "mp").astype(f32), axis=0)
    projected = jnp.einsum("tc,kch->kth", wide_f, embed_proj, precision=highest)
    projected = projected + sum(
        one_hot[:, j][:, None, None]
        * block_terms[:, j * channels : (j + 1) * channels][None]
        for j in range(picked)
    )
    grid = projected.reshape(heads, rows + 4, GRID_W, channels)
    row_id = seq * rows - 2 + jnp.arange(rows + 4)
    inside = ((row_id >= 0) & (row_id < rows * n_seq)).astype(f32)[None, :, None, None]
    conv_field = conv_rows(grid * inside, head_kernel, 1)
    gating = jax.nn.sigmoid(conv_field)
    out_scale = head_out[:, None, None, :]
    logits = jnp.sum((conv_field * gating * out_scale)[:, 1 : rows + 1], -1).reshape(
        1, heads, tokens
    )
    slope_grad = -out_scale * gating * (1.0 + conv_field * (1.0 - gating)) * inside[:, 1:-1]
    field_grad = conv_rows(slope_grad, head_kernel, -1).reshape(heads, tokens, channels)
    field_grad = field_grad.astype(bf16)
    head_part = jnp.einsum("kth,kch->tc", field_grad.astype(f32), embed_proj, precision=highest)
    picked_grad = jnp.concatenate(
        [
            jnp.sum(field_grad * one_hot[:, j][:, None, None].astype(bf16), 0)
            for j in range(picked)
        ],
        axis=1,
    )
    hidden_grad = lax.dot_general(
        picked_grad, out_fold, (((1,), (1,)), ((), ())), preferred_element_type=f32
    )
    own = slice(halo, halo + tokens)
    preact_grad = (hidden_grad * gelu_slope(preact[own])).astype(bf16)
    scaled_back = lax.psum(
        lax.dot_general(
            preact_grad, up_fold, (((1,), (1,)), ((), ())), preferred_element_type=f32
        ),
        "mp",
    )
    noised_f, own_inv = wide_f[own], inv_std[own]
    along = jnp.sum(noised_f * scaled_back, -1, keepdims=True) / width
    latent_grad = retain * (
        (scaled_back - own_inv * own_inv * wide_gram[own] * along) * own_inv + head_part
    )
    return (latents[None], logits, latent_grad[None])


def solution(mesh):
    return jax.shard_map(
        per_device,
        mesh=mesh,
        in_specs=(
            P("group", "seq", "mp"),
            P(None, "seq"),
            P("seq", "group", "mp"),
            P("mp", None),
            P("group"),
            P("group", "seq", None),
            P(None, "mp"),
            P(None, None, "mp"),
            P("seq", "mp"),
            P("mp", "seq"),
            P(None, "mp", None),
            P(),
            P(),
            P("group", None),
        ),
        out_specs=(P("group", "seq", None), P("group", None, "seq"), P("group", "seq", None)),
        check_vma=False,
    )
```

```python
import functools
import math

import jax
import jax.numpy as jnp
from jax import lax
from jax.experimental import pallas as pl
from jax.experimental.pallas import tpu as pltpu
from jax.sharding import PartitionSpec as P

GRID_W = 64


EPSILON = 1e-06
GELU_COEF = 0.7978845608028654


def gelu_tanh(values):
    inner = GELU_COEF * (values + 0.044715 * values * values * values)
    return 0.5 * values * (1.0 + jnp.tanh(inner))


def gelu_slope(values):
    inner = GELU_COEF * (values + 0.044715 * values * values * values)
    tangent = jnp.tanh(inner)
    return 0.5 * (1.0 + tangent) + 0.5 * values * (1.0 - tangent * tangent) * GELU_COEF * (
        1.0 + 3.0 * 0.044715 * values * values
    )


def time_features(timestep, width):
    half_width = width // 2
    index = jnp.arange(half_width, dtype=jnp.float32)
    freqs = jnp.exp(-math.log(10000.0) * index / half_width)
    angles = timestep.astype(jnp.float32)[:, None] * freqs[None, :]
    return jnp.concatenate([jnp.cos(angles), jnp.sin(angles)], axis=-1)


MESH = pl.DeviceIdType.MESH
NEAR = 2
PIECES = 8


def fold_kernel(n_group, n_seq, n_mp, pieces, fold_ref, slim_ref, mod_ref, *refs):
    fold_out, slim_out, mod_out_ref = refs[2:5]
    pair_refs, pair_outs = refs[:2], refs[5:7]
    (
        near_in, part, far_in, slim_near, slim_part, slim_far, mod_in, *pair_in,
        near_sems, far_sems, back_sems, last_sems, mod_sems, pair_sems,
    ) = refs[7:]
    far = n_seq // NEAR
    group, seq, mp = lax.axis_index("group"), lax.axis_index("seq"), lax.axis_index("mp")
    my_far, my_near = seq // NEAR, lax.rem(seq, NEAR)
    other = lax.rem(my_near + 1, NEAR)
    piece = fold_ref.shape[2] // pieces
    share = fold_ref.shape[2]
    half = far * share
    f32 = jnp.float32

    partners = [(dg, ds) for dg in range(n_group) for ds in range(n_seq) if dg or ds]
    barrier = pltpu.get_barrier_semaphore()
    for dg, ds in partners:
        target = {"group": lax.rem(group + dg, n_group), "seq": lax.rem(seq + ds, n_seq)}
        pl.semaphore_signal(barrier, inc=1, device_id=target, device_id_type=MESH)
    for dm in range(1, n_mp):
        target = {"mp": lax.rem(mp + dm, n_mp)}
        pl.semaphore_signal(barrier, inc=1, device_id=target, device_id_type=MESH)
    pl.semaphore_wait(barrier, len(partners) + n_mp - 1)

    def far_id(step):
        return lax.rem(my_far + step, far) * NEAR + my_near

    def lanes(start, size):
        return pl.ds(pl.multiple_of(start, 128), size)

    def rows(s):
        return pl.ds((s - 1) * piece, piece)

    def source(s, near):
        return slim_ref.at[:, lanes(near * half, half)] if s == 0 else fold_ref.at[near, :, rows(s)]

    def from_near(s):
        return slim_near if s == 0 else near_in.at[:, rows(s)]

    def partial(s):
        return slim_part if s == 0 else part.at[:, rows(s)]

    def partial_of(s, z):
        return slim_part.at[:, lanes(z * share, share)] if s == 0 else part.at[z, rows(s)]

    def from_far(s, k):
        return slim_far.at[k - 1] if s == 0 else far_in.at[k - 1, rows(s)]

    def result_of(s):
        if s == 0:
            return slim_out.at[:, lanes(my_near * half + my_far * share, share)]
        return fold_out.at[my_near, my_far, rows(s)]

    def result(s):
        if s == 0:
            return slim_out.at[:, lanes(my_near * half, half)]
        return fold_out.at[my_near, :, rows(s)]

    def send(src, dst, sems, index, target):
        copy = pltpu.make_async_remote_copy(
            src_ref=src,
            dst_ref=dst,
            send_sem=sems.at[(0, *index)],
            recv_sem=sems.at[(1, *index)],
            device_id=target,
            device_id_type=MESH,
        )
        copy.start()
        return copy

    count = pieces + 1
    order = [*range(1, pieces // 2 + 1), 0, *range(pieces // 2 + 1, count)]
    across = {"seq": my_far * NEAR + other}
    near_copies = {
        s: send(source(s, other), from_near(s), near_sems, (s,), across) for s in order
    }
    mod_copies = []
    for dg, ds in partners:
        to_group = lax.rem(group + dg, n_group)
        target = {"group": to_group, "seq": lax.rem(seq + ds, n_seq)}
        mod_copies.append(
            send(mod_ref.at[to_group], mod_in.at[dg, ds], mod_sems, (dg, ds), target)
        )
    pair_copies = [
        send(pair_refs[i], pair_in[i].at[dm], pair_sems, (i, dm), {"mp": lax.rem(mp + dm, n_mp)})
        for i in range(2)
        for dm in range(1, n_mp)
    ]

    far_copies, back_copies, last_copies = {}, {}, {}
    for s in order:
        near_copies[s].wait_recv()
        partial(s)[...] = (
            source(s, my_near)[...].astype(f32) + from_near(s)[...].astype(f32)
        ).astype(part.dtype)
        for k in range(1, far):
            far_copies[s, k] = send(
                partial_of(s, lax.rem(my_far + k, far)),
                from_far(s, k),
                far_sems,
                (s, k - 1),
                {"seq": far_id(k)},
            )

    def finish(s):
        for k in range(1, far):
            back_copies[s, k].wait_recv()
        last_copies[s] = send(result(s), result(s), last_sems, (s,), across)

    for place, s in enumerate(order):
        total = partial_of(s, my_far)[...].astype(f32)
        for k in range(1, far):
            far_copies[s, k].wait_recv()
            total = total + from_far(s, k)[...].astype(f32)
        result_of(s)[...] = total.astype(fold_out.dtype)
        for k in range(1, far):
            back_copies[s, k] = send(
                result_of(s), result_of(s), back_sems, (s, k - 1), {"seq": far_id(k)}
            )
        if place >= 1:
            finish(order[place - 1])
    for copy in mod_copies + pair_copies:
        copy.wait_recv()
    for dg in range(n_group):
        total = mod_ref[group] if dg == 0 else mod_in[dg, 0]
        for ds in range(1, n_seq):
            total = total + mod_in[dg, ds]
        mod_out_ref[lax.rem(group + n_group - dg, n_group)] = total
    for i in range(2):
        total = pair_refs[i][...]
        for dm in range(1, n_mp):
            total = total + pair_in[i][dm]
        pair_outs[i][...] = total
    finish(order[-1])
    for s in order:
        last_copies[s].wait_recv()
    for copies in (near_copies.values(), far_copies.values(), back_copies.values(), last_copies.values()):
        for copy in copies:
            copy.wait_send()
    for copy in mod_copies + pair_copies:
        copy.wait_send()


def summed_folds(fold, slim, mod, pair):
    n_group, n_seq, n_mp = (lax.axis_size(axis) for axis in ("group", "seq", "mp"))
    hidden, columns = fold.shape
    share = hidden // n_seq
    far = n_seq // NEAR
    mod_rows = mod.shape[1] // 128
    fits = hidden % n_seq == 0 and n_seq % NEAR == 0 and far > 1 and share % (16 * PIECES) == 0
    if not fits or share % 128 or mod.shape[1] % 128 or mod.shape[0] != n_group:
        halves = lax.all_gather(lax.psum(mod, "seq"), "group", axis=1)
        own = lax.dynamic_slice_in_dim(halves, lax.axis_index("group"), 1, 0)[0]
        return lax.psum(fold, "seq"), lax.psum(slim, "seq"), own, lax.psum(pair, "mp")
    dma = pltpu.SemaphoreType.DMA
    vmem = pl.BlockSpec(memory_space=pltpu.VMEM)
    tall, kind, height = PIECES + 1, fold.dtype, slim.shape[0]
    summed, slim_sum, own, *pair_sum = pl.pallas_call(
        functools.partial(fold_kernel, n_group, n_seq, n_mp, PIECES),
        out_shape=(
            jax.ShapeDtypeStruct((NEAR, far, share, columns), kind),
            jax.ShapeDtypeStruct(slim.shape, kind),
            jax.ShapeDtypeStruct((n_group, mod_rows, 128), jnp.float32),
            *(jax.ShapeDtypeStruct(value.shape, value.dtype) for value in pair),
        ),
        in_specs=[vmem] * 5,
        out_specs=(vmem,) * 5,
        scratch_shapes=[
            pltpu.VMEM((far, share, columns), kind),
            pltpu.VMEM((far, share, columns), kind),
            pltpu.VMEM((far - 1, share, columns), kind),
            pltpu.VMEM((height, far * share), kind),
            pltpu.VMEM((height, far * share), kind),
            pltpu.VMEM((far - 1, height, share), kind),
            pltpu.VMEM((n_group, n_seq, mod_rows, 128), jnp.float32),
            *(pltpu.VMEM((n_mp, *value.shape), value.dtype) for value in pair),
            dma((2, tall)),
            dma((2, tall, far - 1)),
            dma((2, tall, far - 1)),
            dma((2, tall)),
            dma((2, n_group, n_seq)),
            dma((2, 2, n_mp)),
        ],
        compiler_params=pltpu.CompilerParams(
            collective_id=0, has_side_effects=True, vmem_limit_bytes=40 * 1024 * 1024
        ),
    )(
        fold.reshape(NEAR, far, share, columns),
        slim,
        mod.reshape(mod.shape[0], mod_rows, 128),
        *pair,
    )
    return summed.reshape(hidden, columns), slim_sum, own.reshape(n_group, mod.shape[1]), pair_sum


def shifted(grid, offset):
    zero = jnp.zeros_like(grid[:, :, :1])
    if offset == -1:
        return jnp.concatenate([zero, grid[:, :, :-1]], axis=2)
    if offset == 1:
        return jnp.concatenate([grid[:, :, 1:], zero], axis=2)
    return grid


def conv_rows(grid, kernel, sign):
    rows = grid.shape[1] - 2
    total = None
    moved = {off: shifted(grid, off) for off in (-1, 0, 1)}
    for i in range(3):
        for j in range(3):
            row = 1 + sign * (i - 1)
            term = kernel[:, i, j][:, None, None, :] * moved[sign * (j - 1)][:, row : row + rows]
            total = term if total is None else total + term
    return total


def per_device(
    student_hidden,
    student_cond,
    student_mod,
    student_out,
    timestep,
    noise,
    teacher_embed,
    teacher_mod,
    up_weight,
    down_weight,
    head_proj,
    head_kernel,
    head_out,
    disc_layer,
):
    highest = lax.Precision.HIGHEST
    f32, bf16 = jnp.float32, jnp.bfloat16
    n_mp, n_seq = lax.axis_size("mp"), lax.axis_size("seq")
    seq = lax.axis_index("seq")
    tokens = student_hidden.shape[1]
    rows = tokens // GRID_W
    local_width = student_hidden.shape[2]
    width = local_width * n_mp
    latent_width = noise.shape[2]
    heads, _, channels = head_proj.shape
    picked = heads // 2

    reads = (disc_layer[0] == 1).astype(jnp.int32)
    order = jnp.arange(heads)
    rank = jnp.sum(jnp.where(order[None, :] < order[:, None], reads[None, :], 0), axis=1)
    slot_head = [
        jnp.sum(jnp.where((reads == 1) & (rank == j), jnp.arange(heads), 0)) for j in range(picked)
    ]
    one_hot = jnp.stack(
        [((reads == 1) & (rank == j)).astype(f32) for j in range(picked)], axis=1
    )

    embed_full = lax.all_gather(teacher_embed, "mp", axis=1, tiled=True)
    tmod = jnp.einsum(
        "f,fjd->jd",
        time_features(timestep, teacher_mod.shape[0])[0],
        teacher_mod.astype(f32),
        precision=highest,
    )
    tmod = lax.all_gather(tmod, "mp", axis=1, tiled=True)
    chunk = width // n_seq
    start = seq * chunk
    owner = start // local_width
    offset = start - owner * local_width
    own_proj = jnp.stack(
        [
            lax.dynamic_slice(head_proj, (slot_head[j], offset, 0), (1, chunk, channels))[0]
            for j in range(picked)
        ],
        axis=1,
    ).reshape(chunk, picked * channels)
    own_proj = lax.all_gather(own_proj, "mp")
    proj_chunk = lax.dynamic_index_in_dim(own_proj, owner, 0, keepdims=False)
    out_terms = jnp.dot(down_weight, proj_chunk, preferred_element_type=f32).astype(bf16)
    embed_f = embed_full.astype(f32)
    embed_centered = embed_f - jnp.mean(embed_f, axis=1, keepdims=True)
    gram = jnp.einsum("cd,ed->ce", embed_centered, embed_centered, precision=highest)
    stacked = jnp.concatenate(
        [embed_centered * (1.0 + tmod[1:2]), tmod[0:1]], axis=0
    ).astype(bf16)
    stacked = lax.dynamic_slice_in_dim(stacked, start, chunk, 1)
    pad = -stacked.shape[0] % 16
    stacked = jnp.pad(stacked, ((0, pad), (0, 0)))
    in_terms = jnp.dot(stacked, up_weight, preferred_element_type=f32).astype(bf16)
    embed_proj = jnp.einsum("cd,kdh->kch", teacher_embed, head_proj, preferred_element_type=f32)

    hidden = student_hidden[0].astype(f32)
    token_sums = jnp.stack([jnp.sum(hidden, -1), jnp.sum(hidden * hidden, -1)])
    half_mod = jnp.einsum(
        "sk,kjd->sjd", student_cond, student_mod.astype(f32), precision=highest
    )
    out_fold, in_fold, own_mod, (token_sums, embed_proj) = summed_folds(
        out_terms, in_terms, half_mod[:, 0], (token_sums, embed_proj)
    )
    up_fold = in_fold[:latent_width]
    bias = in_fold[latent_width : latent_width + 1].astype(f32)
    tok_mean = (token_sums[0] / width)[:, None]
    tok_var = (token_sums[1] / width)[:, None] - tok_mean * tok_mean
    normed = (
        (hidden - tok_mean) * lax.rsqrt(tok_var + EPSILON) * (1.0 + own_mod[1:2]) + own_mod[0:1]
    ).astype(bf16)
    latents = lax.psum(
        jnp.dot(normed, student_out, preferred_element_type=f32).astype(bf16), "mp"
    )
    level = timestep[0].astype(f32) / 1000.0
    retain = 1.0 - level
    noised = (retain * latents.astype(f32) + level * noise[0].astype(f32)).astype(bf16)

    halo = 2 * GRID_W
    ups = [(i, i + 1) for i in range(n_seq - 1)]
    downs = [(j, i) for i, j in ups]
    before = lax.ppermute(noised[tokens - halo :], "seq", ups)
    after = lax.ppermute(noised[:halo], "seq", downs)
    wide = jnp.concatenate([before, noised, after], axis=0)

    wide_f = wide.astype(f32)
    wide_gram = jnp.dot(wide_f, gram, precision=highest)
    var_t = jnp.sum(wide_f * wide_gram, -1, keepdims=True) / width
    inv_std = lax.rsqrt(var_t + EPSILON)
    preact = inv_std * jnp.dot(wide, up_fold, preferred_element_type=f32) + bias
    activated = gelu_tanh(preact).astype(bf16)
    block_terms = jnp.dot(activated, out_fold, preferred_element_type=f32).astype(bf16)
    block_terms = jnp.sum(lax.all_gather(block_terms, "mp").astype(f32), axis=0)
    projected = jnp.einsum("tc,kch->kth", wide_f, embed_proj, precision=highest)
    projected = projected + sum(
        one_hot[:, j][:, None, None]
        * block_terms[:, j * channels : (j + 1) * channels][None]
        for j in range(picked)
    )
    grid = projected.reshape(heads, rows + 4, GRID_W, channels)
    row_id = seq * rows - 2 + jnp.arange(rows + 4)
    inside = ((row_id >= 0) & (row_id < rows * n_seq)).astype(f32)[None, :, None, None]
    conv_field = conv_rows(grid * inside, head_kernel, 1)
    gating = jax.nn.sigmoid(conv_field)
    out_scale = head_out[:, None, None, :]
    logits = jnp.sum((conv_field * gating * out_scale)[:, 1 : rows + 1], -1).reshape(
        1, heads, tokens
    )
    slope_grad = -out_scale * gating * (1.0 + conv_field * (1.0 - gating)) * inside[:, 1:-1]
    field_grad = conv_rows(slope_grad, head_kernel, -1).reshape(heads, tokens, channels)
    field_grad = field_grad.astype(bf16)
    head_part = jnp.einsum("kth,kch->tc", field_grad.astype(f32), embed_proj, precision=highest)
    picked_grad = jnp.concatenate(
        [
            jnp.sum(field_grad * one_hot[:, j][:, None, None].astype(bf16), 0)
            for j in range(picked)
        ],
        axis=1,
    )
    hidden_grad = lax.dot_general(
        picked_grad, out_fold, (((1,), (1,)), ((), ())), preferred_element_type=f32
    )
    own = slice(halo, halo + tokens)
    preact_grad = (hidden_grad * gelu_slope(preact[own])).astype(bf16)
    scaled_back = lax.psum(
        lax.dot_general(
            preact_grad, up_fold, (((1,), (1,)), ((), ())), preferred_element_type=f32
        ),
        "mp",
    )
    noised_f, own_inv = wide_f[own], inv_std[own]
    along = jnp.sum(noised_f * scaled_back, -1, keepdims=True) / width
    latent_grad = retain * (
        (scaled_back - own_inv * own_inv * wide_gram[own] * along) * own_inv + head_part
    )
    return (latents[None], logits, latent_grad[None])


def solution(mesh):
    return jax.shard_map(
        per_device,
        mesh=mesh,
        in_specs=(
            P("group", "seq", "mp"),
            P(None, "seq"),
            P("seq", "group", "mp"),
            P("mp", None),
            P("group"),
            P("group", "seq", None),
            P(None, "mp"),
            P(None, None, "mp"),
            P("seq", "mp"),
            P("mp", "seq"),
            P(None, "mp", None),
            P(),
            P(),
            P("group", None),
        ),
        out_specs=(P("group", "seq", None), P("group", None, "seq"), P("group", "seq", None)),
        check_vma=False,
    )
```
